32 devices in a mesh: seq: 8 (over z, x), tp: 4 (over y, core).
Axes of the slice: x: 2, y: 2, z: 4, core: 2. Of those that a mesh axis runs over, the one named last changes fastest.
Arguments:
- state: bfloat16 [2304, 3072], P('seq', 'tp'), may hold values from -40 to 40
- latent: float32 [1152, 64], P('seq'), may hold values from -6 to 6
- w_mod: bfloat16 [3072, 9216], P('tp', 'seq'), may hold values from -0.109375 to 0.109375
- w_qkv: bfloat16 [3072, 3, 1536], P(None, None, 'tp'), may hold values from -1 to 1
- w_mlp_in: bfloat16 [3072, 6144], P('seq', 'tp'), may hold values from -0.109375 to 0.109375
- q_gain: float32 [12, 128], P('tp'), may hold values from 1.4 to 6.6
- k_gain: float32 [12, 128], P('tp'), may hold values from 1.4 to 6.6
- w_out: bfloat16 [1536, 3072], P('tp'), may hold values from -0.15625 to 0.15625
- w_mlp_down: bfloat16 [3072, 6144], P('seq', 'tp'), may hold values from -0.078125 to 0.078125
- w_final: bfloat16 [3072, 64], P('tp'), may hold values from -0.109375 to 0.109375
- text_len: int32 [2, 2], replicated, may hold values from 64 to 512, as said below
- rope_ids: int32 [3, 2304], P(None, 'seq'), may hold values from 0 to 126, as said below
- guidance: int32 [2], replicated, may hold values from 2 to 12
- step_index: int32 [2], replicated, may hold values from 0 to 27
Outputs:
- new_state: bfloat16 [2304, 3072], P('seq', 'tp')
- next_latent: float32 [1152, 64], P('seq')
- state_norm: float32 [2], replicated
- top_score: float32 [2], replicated
The draws below stay inside these ranges and needn't reach their ends.
Inputs may be any that keep to these rules, and one draw needn't show every extreme that they name: `text_len`: one of the entries equals 512, a different one from draw to draw. `rope_ids`: text positions have ids (0, 0, 0); image position p >= 512 has (frame, row offset + (p - 512) // 64, column offset + (p - 512) % 64), with a frame of 0 or 1 and offsets of 0 to 63 for each request, the same in both halves; one request has row offset 63 and one has column offset 63.
All inputs are finite; a program needn't handle non-finite values.
Results may differ from the reference program's by a relative error of at most 0.008.
Values may be sent and summed in bfloat16 or wider, within the bound.
A program may use at most 192 MiB of HBM per device.

```python
import math
import jax
import jax.numpy as jnp
from jax import lax

D = 3072
HD = 128
CH = 64
HEADS = 12
FF = 6144
REQ = 2
TOK_DEV = 288
TXT = 512
IMG_W = 64
STEPS = 28
BLOCKS = 2
SEQ_LEN = 576
SEQ_ROWS = 2304


def draw_state(key, part):
    ramp = jnp.arange(SEQ_ROWS, dtype=jnp.float32) / SEQ_ROWS
    rough = jnp.clip(jax.random.normal(jax.random.fold_in(key, 1), (SEQ_ROWS, D), jnp.float32), -5.0, 5.0)
    values = rough * (0.5 + ramp)[:, None]
    return values.astype(jnp.bfloat16)


def draw_w_qkv(key, part):
    base = jnp.clip(jax.random.normal(jax.random.fold_in(key, 1), (D, 3, HEADS * HD), jnp.float32), -5.0, 5.0) / math.sqrt(D)
    return base.astype(jnp.bfloat16)


def gain_table(key, salt):
    return jax.random.uniform(jax.random.fold_in(key, salt), (HEADS, HD), jnp.float32, 1.4, 2.6)


def draw_q_gain(key, part):
    return gain_table(key, 11)


def draw_k_gain(key, part):
    return gain_table(key, 21)


def draw_text_len(key, part):
    lengths = jax.random.randint(jax.random.fold_in(key, 1), (REQ * 2,), TXT // 8, TXT + 1)
    chosen = jax.random.randint(jax.random.fold_in(key, 2), (), 0, REQ * 2)
    lengths = jnp.where(jnp.arange(REQ * 2) == chosen, TXT, lengths)
    return lengths.reshape(REQ, 2).astype(jnp.int32)


def offset_pair(key, salt):
    free_value = jax.random.randint(jax.random.fold_in(key, salt), (), 0, 64)
    flipped = jax.random.randint(jax.random.fold_in(key, salt + 1), (), 0, 2)
    first_req = jnp.where(flipped == 1, free_value, 63)
    second_req = jnp.where(flipped == 1, 63, free_value)
    return jnp.stack([first_req, second_req] + [free_value] * (REQ - 2)).astype(jnp.int32)


def draw_rope_ids(key, part):
    row_index = jnp.arange(SEQ_ROWS, dtype=jnp.int32)
    within = row_index % TOK_DEV
    block_id = row_index // (2 * TOK_DEV) % BLOCKS
    request_id = row_index // (2 * TOK_DEV * BLOCKS)
    position = block_id * TOK_DEV + within
    image_part = position >= TXT
    relative = jnp.maximum(position - TXT, 0)
    row_offsets = offset_pair(key, 10)
    col_offsets = offset_pair(key, 20)
    frames = jax.random.randint(jax.random.fold_in(key, 30), (REQ,), 0, 2)
    picker = (request_id[:, None] == jnp.arange(REQ, dtype=jnp.int32)[None, :]).astype(jnp.int32)
    frame_tok = jnp.sum(picker * frames[None, :], axis=1)
    row_tok = jnp.sum(picker * row_offsets[None, :], axis=1) + relative // IMG_W
    col_tok = jnp.sum(picker * col_offsets[None, :], axis=1) + relative % IMG_W
    stacked = jnp.stack([frame_tok, row_tok, col_tok], axis=0)
    return jnp.where(image_part[None, :], stacked, 0).astype(jnp.int32)


def levels(stream_key, extent, shards, smallest, high):
    def one(dim, blocks):
        draws = jax.random.uniform(jax.random.fold_in(jax.random.fold_in(stream_key, 6), dim), (blocks,), jnp.float32, smallest / len(shards), high / len(shards))
        return jnp.repeat(jnp.exp(draws), extent[dim] // blocks).reshape((-1,) + (1,) * (len(extent) - dim - 1))

    loudness = one(*shards[0])
    for cut in shards[1:]:
        loudness = loudness * one(*cut)
    return loudness


def scatter_about(stream_key, extent, scale, bound, split=(), held_as=jnp.bfloat16):
    values = scale * jax.random.normal(stream_key, extent, jnp.float32)
    if split:
        values = values * levels(stream_key, extent, split, -0.22, 0.18)
    return jnp.clip(values, -bound, bound).astype(held_as)


def setup_inputs(seed: int = 0) -> dict:
    seeds = jax.random.split(jax.random.key(seed), 15)
    state = draw_state(jax.random.fold_in(seeds[14], 71), 0)
    latent = scatter_about(seeds[1], (REQ * SEQ_LEN, CH), 1.0, 6.0, ((0, 8),), jnp.float32)
    w_mod = scatter_about(seeds[2], (D, 3 * D), D ** -0.5, 0.109375, ((0, 4), (1, 8)))
    w_qkv = draw_w_qkv(jax.random.fold_in(seeds[14], 71), 0)
    w_mlp_in = scatter_about(seeds[4], (D, FF), D ** -0.5, 0.109375, ((0, 8), (1, 4)))
    q_gain = draw_q_gain(jax.random.fold_in(seeds[14], 71), 0)
    k_gain = draw_k_gain(jax.random.fold_in(seeds[14], 71), 0)
    w_out = scatter_about(seeds[7], (HEADS * HD, D), (HEADS * HD) ** -0.5, 0.15625, ((0, 4),))
    w_mlp_down = scatter_about(seeds[8], (D, FF), FF ** -0.5, 0.078125, ((0, 8), (1, 4)))
    w_final = scatter_about(seeds[9], (D, CH), D ** -0.5, 0.109375, ((0, 4),))
    text_len = draw_text_len(jax.random.fold_in(seeds[14], 71), 0)
    rope_ids = draw_rope_ids(jax.random.fold_in(seeds[14], 71), 0)
    guidance = jax.random.randint(seeds[12], (REQ,), 2, 13).astype(jnp.int32)
    step_index = jax.random.randint(seeds[13], (REQ,), 0, STEPS).astype(jnp.int32)
    return dict(state=state, latent=latent, w_mod=w_mod, w_qkv=w_qkv, w_mlp_in=w_mlp_in, q_gain=q_gain, k_gain=k_gain, w_out=w_out, w_mlp_down=w_mlp_down, w_final=w_final, text_len=text_len, rope_ids=rope_ids, guidance=guidance, step_index=step_index)


TIME_SHIFT = 1.15
ROPE_THETA = 10000.0
NORM_EPS = 1e-06
MASKED_SCORE = -1e+30

def sigma_of(step_count):
    fraction = 1.0 - step_count.astype(jnp.float32) / STEPS
    boosted = math.exp(TIME_SHIFT) * fraction
    return boosted / (boosted + 1.0 - fraction)

def time_embedding(sigma_vals):
    half_width = D // 2
    frequency = jnp.exp(-math.log(10000.0) * jnp.arange(half_width, dtype=jnp.float32) / half_width)
    phases = 1000.0 * sigma_vals[:, None] * frequency[None, :]
    return jnp.concatenate([jnp.cos(phases), jnp.sin(phases)], axis=1)

def layer_norm(rows):
    center = lax.optimization_barrier(jnp.mean(rows, axis=-1, keepdims=True))
    spread = lax.optimization_barrier(jnp.mean(jnp.square(rows - center), axis=-1, keepdims=True))
    return (rows - center) * lax.rsqrt(spread + NORM_EPS)

def rms_norm(rows):
    return rows * lax.rsqrt(lax.optimization_barrier(jnp.mean(jnp.square(rows), axis=-1, keepdims=True)) + NORM_EPS)

def rope_angles(id_rows):
    pieces = []
    for component, width in enumerate((HD // 8, 7 * HD // 16, 7 * HD // 16)):
        index_vec = jnp.arange(width // 2, dtype=jnp.float32)
        omega = jnp.exp(-math.log(ROPE_THETA) * 2.0 * index_vec / width)
        pieces.append(id_rows[component].astype(jnp.float32)[:, None] * omega[None, :])
    return jnp.concatenate(pieces, axis=1)

def rotate(rows, angles):
    count, heads_here, size = rows.shape
    paired = rows.reshape(count, heads_here, size // 2, 2)
    cosine = jnp.cos(angles)[:, None, :]
    sine = jnp.sin(angles)[:, None, :]
    first = paired[..., 0]
    second = paired[..., 1]
    turned = jnp.stack([first * cosine - second * sine, first * sine + second * cosine], axis=-1)
    return turned.reshape(count, heads_here, size)

def reference(state, latent, w_mod, w_qkv, w_mlp_in, q_gain, k_gain, w_out, w_mlp_down, w_final, text_len, rope_ids, guidance, step_index):
    sigma_now = sigma_of(step_index)
    step_size = sigma_of(step_index + 1) - sigma_now
    time_vec = jax.nn.silu(time_embedding(sigma_now)).astype(jnp.bfloat16)
    modulation = jnp.dot(time_vec, w_mod, preferred_element_type=jnp.float32)
    grouped = state.reshape(REQ, BLOCKS, 2, TOK_DEV, D).transpose(0, 2, 1, 3, 4).reshape(REQ, 2, SEQ_LEN, D)
    id_grid = rope_ids.reshape(3, REQ, BLOCKS, 2, TOK_DEV).transpose(0, 1, 3, 2, 4).reshape(3, REQ, 2, SEQ_LEN)
    positions = jnp.arange(SEQ_LEN, dtype=jnp.int32)
    weight_flat = w_qkv.reshape(D, 3 * HEADS * HD)
    score_scale = 1.0 / math.sqrt(HD)
    latent_rows = latent.reshape(REQ, SEQ_LEN, CH)
    state_parts = []
    latent_parts = []
    square_list = []
    peak_list = []
    for request in range(REQ):
        shift_vec = modulation[request, :D]
        scale_vec = modulation[request, D:2 * D]
        gate_vec = modulation[request, 2 * D:]
        half_states = []
        half_velocity = []
        square_total = jnp.zeros((), jnp.float32)
        peak_total = jnp.full((), MASKED_SCORE, jnp.float32)
        for guided_half in range(2):
            rows = grouped[request, guided_half].astype(jnp.float32)
            modded = ((1.0 + scale_vec) * layer_norm(rows) + shift_vec).astype(jnp.bfloat16)
            projected = jnp.dot(modded, weight_flat, preferred_element_type=jnp.float32).reshape(SEQ_LEN, 3, HEADS, HD)
            mlp_pre = jnp.dot(modded, w_mlp_in, preferred_element_type=jnp.float32)
            mlp_hidden = jax.nn.gelu(mlp_pre, approximate=True).astype(jnp.bfloat16)
            angles = rope_angles(id_grid[:, request, guided_half])
            queries = rotate(rms_norm(projected[:, 0]) * q_gain[None], angles).astype(jnp.bfloat16)
            key_rows = rotate(rms_norm(projected[:, 1]) * k_gain[None], angles).astype(jnp.bfloat16)
            value_rows = projected[:, 2].astype(jnp.bfloat16)
            live = (positions >= TXT) | (positions < text_len[request, guided_half])

            def one_head(operands):
                head_queries, head_keys, head_values = operands
                scores = jnp.dot(head_queries, head_keys.T, preferred_element_type=jnp.float32) * score_scale
                scores = jnp.where(live[None, :], scores, MASKED_SCORE)
                row_max = lax.optimization_barrier(jnp.max(scores, axis=1, keepdims=True))
                weights = jnp.exp(scores - row_max)
                weights = (weights / lax.optimization_barrier(jnp.sum(weights, axis=1, keepdims=True))).astype(jnp.bfloat16)
                result = jnp.dot(weights, head_values, preferred_element_type=jnp.float32).astype(jnp.bfloat16)
                return (result, jnp.max(row_max))
            attended, head_peaks = lax.map(one_head, (queries.transpose(1, 0, 2), key_rows.transpose(1, 0, 2), value_rows.transpose(1, 0, 2)))
            attended = attended.transpose(1, 0, 2).reshape(SEQ_LEN, HEADS * HD)
            update = jnp.dot(attended, w_out, preferred_element_type=jnp.float32) + jnp.dot(mlp_hidden, w_mlp_down.T, preferred_element_type=jnp.float32)
            new_half = (rows + gate_vec * update).astype(jnp.bfloat16)
            new_values = new_half.astype(jnp.float32)
            normed_out = layer_norm(new_values).astype(jnp.bfloat16)
            half_velocity.append(jnp.dot(normed_out, w_final, preferred_element_type=jnp.float32))
            half_states.append(new_half)
            square_total = square_total + jnp.sum(new_values * new_values)
            peak_total = jnp.maximum(peak_total, jnp.max(head_peaks))
        guide_scale = guidance[request].astype(jnp.float32) / 2.0
        guided = half_velocity[1] + guide_scale * (half_velocity[0] - half_velocity[1])
        latent_parts.append(latent_rows[request] + step_size[request] * guided)
        state_parts.append(jnp.stack(half_states, axis=0))
        square_list.append(square_total)
        peak_list.append(peak_total)
    new_state = jnp.stack(state_parts, axis=0).reshape(REQ, 2, BLOCKS, TOK_DEV, D).transpose(0, 2, 1, 3, 4).reshape(SEQ_ROWS, D)
    next_latent = jnp.stack(latent_parts, axis=0).reshape(REQ * SEQ_LEN, CH)
    state_norm = jnp.sqrt(jnp.stack(square_list) / (2.0 * SEQ_LEN * D))
    top_score = jnp.stack(peak_list)
    return (new_state, next_latent, state_norm, top_score)
```

```python
import math

import jax
import jax.numpy as jnp
from jax import lax
from jax.sharding import PartitionSpec as P

D = 3072
HD = 128
REQ = 2
TOK_DEV = 288
TXT = 512
STEPS = 28


TIME_SHIFT = 1.15
ROPE_THETA = 10000.0
NORM_EPS = 1e-06
MASKED_SCORE = -1e30


def partner(value, axis, apart):
    return lax.ppermute(value, axis, [(i, i ^ 1 << apart) for i in range(lax.axis_size(axis))])


def crossed(value, axis, mask):
    pairs = [(i, i ^ mask) for i in range(lax.axis_size(axis))]
    return jax.tree.map(lambda part: lax.ppermute(part, axis, pairs), value)


def summed(value, axis):
    mask = 1
    while mask < lax.axis_size(axis):
        value = jax.tree.map(jnp.add, value, crossed(value, axis, mask))
        mask *= 2
    return value


def placed(pieces, index, count):
    shape = pieces[0].shape
    buffer = jnp.zeros((count,) + shape, pieces[0].dtype)
    for mask, piece in pieces.items():
        buffer = lax.dynamic_update_slice(
            buffer, piece[None], (index ^ mask,) + (0,) * len(shape)
        )
    return buffer


def spread(pieces, axis, mask):
    while mask:
        for held in list(pieces):
            pieces[held | mask] = crossed(pieces[held], axis, mask)
        mask //= 2
    return pieces


def gathered_small(value, axis):
    count = lax.axis_size(axis)
    return placed(spread({0: value}, axis, count // 2), lax.axis_index(axis), count)


def gathered_half(weight, axis):
    count = lax.axis_size(axis)
    index = lax.axis_index(axis)
    top = count // 2
    side = index // top
    width = weight.shape[1] // 2
    keep = lax.dynamic_slice_in_dim(weight, side * width, width, 1)
    give = lax.dynamic_slice_in_dim(weight, (1 - side) * width, width, 1)
    pieces = spread({0: keep, top: crossed(give, axis, top)}, axis, top // 2)
    return placed(pieces, index, count).reshape(count * weight.shape[0], width)


def scattered(term, axis):
    index = lax.axis_index(axis)
    core, side = index % 2, index // 2
    quarters = jnp.split(term, 4, axis=1)
    keep = [jnp.where(core == 0, quarters[i], quarters[i + 1]) for i in (0, 2)]
    give = [
        jnp.where(core == 0, quarters[i + 1], quarters[i]).astype(jnp.bfloat16) for i in (0, 2)
    ]
    got = crossed(give, axis, 1)
    low, high = [mine + other.astype(jnp.float32) for mine, other in zip(keep, got)]
    give = jnp.where(side == 0, high, low).astype(jnp.bfloat16)
    return jnp.where(side == 0, low, high) + crossed(give, axis, 2).astype(jnp.float32)


def sigma_of(step_count):
    fraction = 1.0 - step_count.astype(jnp.float32) / STEPS
    boosted = math.exp(TIME_SHIFT) * fraction
    return boosted / (boosted + 1.0 - fraction)


def time_embedding(sigma_vals):
    half_width = D // 2
    frequency = jnp.exp(-math.log(10000.0) * jnp.arange(half_width, dtype=jnp.float32) / half_width)
    phases = 1000.0 * sigma_vals[:, None] * frequency[None, :]
    return jnp.concatenate([jnp.cos(phases), jnp.sin(phases)], axis=1)


def layer_norm(rows):
    center = jnp.mean(rows, axis=-1, keepdims=True)
    spread = jnp.mean(jnp.square(rows - center), axis=-1, keepdims=True)
    return (rows - center) * lax.rsqrt(spread + NORM_EPS)


def rms_norm(rows):
    return rows * lax.rsqrt(jnp.mean(jnp.square(rows), axis=-1, keepdims=True) + NORM_EPS)


def rope_angles(id_rows):
    pieces = []
    for component, width in enumerate((HD // 8, 7 * HD // 16, 7 * HD // 16)):
        index_vec = jnp.arange(width // 2, dtype=jnp.float32)
        omega = jnp.exp(-math.log(ROPE_THETA) * 2.0 * index_vec / width)
        pieces.append(id_rows[component].astype(jnp.float32)[:, None] * omega[None, :])
    return jnp.concatenate(pieces, axis=1)


def rotate(rows, angles):
    count, heads_here, size = rows.shape
    paired = rows.reshape(count, heads_here, size // 2, 2)
    cosine = jnp.cos(angles)[:, None, :]
    sine = jnp.sin(angles)[:, None, :]
    first = paired[..., 0]
    second = paired[..., 1]
    turned = jnp.stack([first * cosine - second * sine, first * sine + second * cosine], axis=-1)
    return turned.reshape(count, heads_here, size)


def down_product(hidden_rows, weight_rows):
    return lax.dot_general(
        hidden_rows, weight_rows, (((1,), (1,)), ((), ())), preferred_element_type=jnp.float32
    )


def body(
    state,
    latent,
    w_mod,
    w_qkv,
    w_mlp_in,
    q_gain,
    k_gain,
    w_out,
    w_mlp_down,
    w_final,
    text_len,
    rope_ids,
    guidance,
    step_index,
):
    blocks = lax.axis_size("seq") // (2 * REQ)
    seq_len = TOK_DEV * blocks
    seq_index = lax.axis_index("seq")
    tp_index = lax.axis_index("tp")
    request = seq_index // (2 * blocks)
    block = seq_index // 2 % blocks
    guided_half = seq_index % 2
    width_tp = state.shape[1]
    request_pick = jnp.arange(REQ, dtype=jnp.int32) == request
    sigma_now = sigma_of(step_index)
    step_size = sigma_of(step_index + 1) - sigma_now
    time_vec = jax.nn.silu(time_embedding(sigma_now)).astype(jnp.bfloat16)
    time_rows = lax.dynamic_slice_in_dim(time_vec, tp_index * width_tp, width_tp, 1)
    partial_mod = jnp.dot(time_rows, w_mod, preferred_element_type=jnp.float32)
    final_total = jnp.sum(w_final.astype(jnp.float32), axis=0)
    summed_mod, final_total = summed((partial_mod, final_total), "tp")
    modulation = gathered_small(summed_mod, "seq").transpose(1, 0, 2).reshape(REQ, 3 * D)
    own_mod = jnp.sum(jnp.where(request_pick[:, None], modulation, 0.0), axis=0)
    far_mod = jnp.sum(jnp.where(request_pick[:, None], 0.0, modulation), axis=0)
    gate_vec = lax.dynamic_slice_in_dim(own_mod[2 * D :], tp_index * width_tp, width_tp, 0)
    far_bit = lax.axis_size("seq") // 2
    far_state = crossed(state, "seq", far_bit)

    def modulated(part, vec):
        rows = lax.all_gather(part, "tp", axis=1, tiled=True).astype(jnp.float32)
        return ((1.0 + vec[D : 2 * D]) * layer_norm(rows) + vec[:D]).astype(jnp.bfloat16)

    modded = modulated(state, own_mod)
    far_modded = modulated(far_state, far_mod)
    heads_here = w_qkv.shape[2] // HD
    projected = jnp.dot(
        modded, w_qkv.reshape(D, 3 * heads_here * HD), preferred_element_type=jnp.float32
    )
    projected = projected.reshape(TOK_DEV, 3, heads_here, HD)
    mlp_pre = jnp.dot(
        jnp.concatenate([far_modded, modded], axis=0),
        gathered_half(w_mlp_in, "seq"),
        preferred_element_type=jnp.float32,
    )
    mlp_hidden = jax.nn.gelu(mlp_pre, approximate=True).astype(jnp.bfloat16)
    down_rows = gathered_half(w_mlp_down, "seq")
    far_term = down_product(mlp_hidden[:TOK_DEV], down_rows)
    mlp_term = down_product(mlp_hidden[TOK_DEV:], down_rows)
    far_update = crossed(scattered(far_term, "tp").astype(jnp.bfloat16), "seq", far_bit)
    angles = rope_angles(rope_ids)
    queries = rotate(rms_norm(projected[:, 0]) * q_gain[None], angles).astype(jnp.bfloat16)
    key_rows = rotate(rms_norm(projected[:, 1]) * k_gain[None], angles).astype(jnp.bfloat16)
    value_rows = projected[:, 2].astype(jnp.bfloat16)
    positions = block * TOK_DEV + jnp.arange(TOK_DEV, dtype=jnp.int32)
    bit_count = blocks.bit_length() - 1
    levels = range(bit_count)
    for level in levels:
        other_keys, other_values = partner((key_rows, value_rows), "seq", level + 1)
        flip_bit = block // 2**level % 2
        other_positions = positions + (1 - 2 * flip_bit) * 2**level * TOK_DEV
        key_rows = jnp.concatenate([key_rows, other_keys], axis=0)
        value_rows = jnp.concatenate([value_rows, other_values], axis=0)
        positions = jnp.concatenate([positions, other_positions], axis=0)
    flat_len = text_len.reshape(2 * REQ)
    own_len = jnp.sum(
        jnp.where(jnp.arange(2 * REQ, dtype=jnp.int32) == request * 2 + guided_half, flat_len, 0)
    )
    live = (positions >= TXT) | (positions < own_len)
    scores = jnp.einsum("qhd,khd->hqk", queries, key_rows, preferred_element_type=jnp.float32) * (
        1.0 / math.sqrt(HD)
    )
    scores = jnp.where(live[None, None, :], scores, MASKED_SCORE)
    row_max = jnp.max(scores, axis=2, keepdims=True)
    top_local = jnp.max(row_max)
    weights = jnp.exp(scores - row_max)
    weights = (weights / jnp.sum(weights, axis=2, keepdims=True)).astype(jnp.bfloat16)
    attended = jnp.einsum("hqk,khd->qhd", weights, value_rows, preferred_element_type=jnp.float32)
    attended = attended.astype(jnp.bfloat16).reshape(TOK_DEV, heads_here * HD)
    term = jnp.dot(attended, w_out, preferred_element_type=jnp.float32) + mlp_term
    update = scattered(term, "tp") + far_update.astype(jnp.float32)
    new_state = (state.astype(jnp.float32) + gate_vec * update).astype(jnp.bfloat16)
    state_values = new_state.astype(jnp.float32)
    row_total = jnp.sum(state_values, axis=1, keepdims=True)
    row_squares = jnp.sum(state_values * state_values, axis=1, keepdims=True)
    raw_velocity = jnp.dot(new_state, w_final, preferred_element_type=jnp.float32)
    tail = jnp.concatenate(
        [raw_velocity, row_total, row_squares, jnp.zeros((TOK_DEV, 62), jnp.float32)], axis=1
    )
    tail = summed(tail, "tp")
    channels = w_final.shape[1]
    row_mean = tail[:, channels : channels + 1] / D
    row_squares = tail[:, channels + 1 : channels + 2]
    row_var = row_squares / D - row_mean * row_mean
    velocity = (tail[:, :channels] - row_mean * final_total) * lax.rsqrt(row_var + NORM_EPS)
    half_rows = TOK_DEV // 2
    keep_part = lax.dynamic_slice_in_dim(velocity, guided_half * half_rows, half_rows, 0)
    give_part = lax.dynamic_slice_in_dim(velocity, (1 - guided_half) * half_rows, half_rows, 0)
    taken_part = partner(give_part.astype(jnp.bfloat16), "seq", 0).astype(give_part.dtype)
    cond_part = jnp.where(guided_half == 0, keep_part, taken_part)
    uncond_part = jnp.where(guided_half == 0, taken_part, keep_part)
    guide_scale = jnp.sum(jnp.where(request_pick, guidance, 0)).astype(jnp.float32) / 2.0
    own_step = jnp.sum(jnp.where(request_pick, step_size, 0.0))
    next_latent = latent + own_step * (uncond_part + guide_scale * (cond_part - uncond_part))
    square_total = summed(jnp.where(request_pick, jnp.sum(row_squares), 0.0), "seq")
    top_score = jnp.where(request_pick, top_local, MASKED_SCORE)
    for axis in ("tp", "seq"):
        mask = 1
        while mask < lax.axis_size(axis):
            top_score = jnp.maximum(top_score, crossed(top_score, axis, mask))
            mask *= 2
    state_norm = jnp.sqrt(square_total / (2.0 * seq_len * D))
    return (new_state, next_latent, state_norm, top_score)


def solution(mesh):
    in_specs = (
        P("seq", "tp"),
        P("seq", None),
        P("tp", "seq"),
        P(None, None, "tp"),
        P("seq", "tp"),
        P("tp", None),
        P("tp", None),
        P("tp", None),
        P("seq", "tp"),
        P("tp", None),
        P(),
        P(None, "seq"),
        P(),
        P(),
    )
    out_specs = (P("seq", "tp"), P("seq", None), P(), P())
    return jax.shard_map(body, mesh=mesh, in_specs=in_specs, out_specs=out_specs, check_vma=False)
```

```python
import functools
import math

import jax
import jax.numpy as jnp
from jax import lax
from jax.experimental import pallas as pl
from jax.experimental.pallas import tpu as pltpu
from jax.sharding import PartitionSpec as P

D = 3072
HD = 128
REQ = 2
TOK_DEV = 288
TXT = 512
STEPS = 28


TIME_SHIFT = 1.15
ROPE_THETA = 10000.0
NORM_EPS = 1e-06
MASKED_SCORE = -1e30


def partner(value, axis, apart):
    return lax.ppermute(value, axis, [(i, i ^ 1 << apart) for i in range(lax.axis_size(axis))])


def crossed(value, axis, mask):
    pairs = [(i, i ^ mask) for i in range(lax.axis_size(axis))]
    return jax.tree.map(lambda part: lax.ppermute(part, axis, pairs), value)


def summed(value, axis):
    mask = 1
    while mask < lax.axis_size(axis):
        value = jax.tree.map(jnp.add, value, crossed(value, axis, mask))
        mask *= 2
    return value


def head_kernel(
    n, w_in, w_down, state, mod, in_all, down_half, rows, far, mod_all, mod_parts,
    own_sem, w_send, w_recv, s_send, s_recv, m_send, m_recv,
):
    seq, tp = lax.axis_index("seq"), lax.axis_index("tp")
    top = n // 2
    side = seq // top
    width = w_in.shape[1] // 2
    depth = state.shape[1]
    bits = [1 << k for k in reversed(range(n.bit_length() - 1))]

    def column(index, size):
        return pl.ds(pl.multiple_of(index * size, size), size)

    def remote(src, dst, send, recv, to_seq, to_tp):
        return pltpu.make_async_remote_copy(
            src_ref=src, dst_ref=dst, send_sem=send, recv_sem=recv,
            device_id=(to_seq, to_tp), device_id_type=pl.DeviceIdType.MESH,
        )

    barrier = pltpu.get_barrier_semaphore()
    for bit in bits:
        pl.semaphore_signal(
            barrier, device_id=(seq ^ bit, tp), device_id_type=pl.DeviceIdType.MESH
        )
    for other in (1, 2, 3):
        pl.semaphore_signal(
            barrier, device_id=(seq, tp ^ other), device_id_type=pl.DeviceIdType.MESH
        )
    pl.semaphore_wait(barrier, len(bits) + 3)

    started = []

    def go(copy):
        copy.start()
        started.append(copy)
        return copy

    def slot(which, mask):
        return in_all.at[seq ^ mask] if which == 0 else down_half.at[(seq ^ mask) // 2]

    def send_piece(which, mask, bit, src):
        return go(
            remote(
                src, slot(which, mask), w_send.at[which, mask, bit.bit_length() - 1],
                w_recv.at[which, mask | bit], seq ^ bit, tp,
            )
        )

    def lowest(which):
        return (1, 2)[which]

    def forward(which, mask, src, below):
        for bit in bits:
            if lowest(which) <= bit < below:
                send_piece(which, mask, bit, src)

    for other in (1, 2, 3):
        go(remote(mod, mod_parts.at[other], m_send.at[other], m_recv.at[other], seq, tp ^ other))
    go(remote(state, far.at[:, column(tp, depth)], s_send.at[4], s_recv.at[4], seq ^ top, tp))
    for other in (1, 2, 3):
        go(
            remote(
                state, rows.at[:, column(tp, depth)], s_send.at[other], s_recv.at[other],
                seq, tp ^ other,
            )
        )
    weights = (w_in, w_down)
    for which in (0, 1):
        far_half = weights[which].at[:, column(1 - side, width)]
        near_half = weights[which].at[:, column(side, width)]
        go_far = remote(
            far_half, slot(which, 0), w_send.at[which, 0, top.bit_length() - 1],
            w_recv.at[which, top], seq ^ top, tp,
        )
        go(go_far)
        forward(which, 0, near_half, top)
    local = [
        pltpu.make_async_copy(
            weights[which].at[:, column(side, width)], slot(which, 0), own_sem.at[which]
        )
        for which in (0, 1)
    ]
    local.append(
        pltpu.make_async_copy(state, rows.at[:, column(tp, depth)], own_sem.at[2])
    )
    for copy in local:
        copy.start()

    total = mod[...]
    for other in (1, 2, 3):
        part = mod_parts.at[other]
        remote(mod, part, m_send.at[other], m_recv.at[other], seq, tp ^ other).wait_recv()
        total = total + mod_parts[other]
    mod_all[seq] = total
    for level in range(n.bit_length() - 1):
        size = 1 << level
        mine = mod_all.at[pl.ds(seq // size * size, size)]
        theirs = mod_all.at[pl.ds((seq ^ size) // size * size, size)]
        go(remote(mine, mine, m_send.at[4 + level], m_recv.at[4 + level], seq ^ size, tp))
        remote(
            mine, theirs, m_send.at[4 + level], m_recv.at[4 + level], seq ^ size, tp
        ).wait_recv()

    def arrive(which, mask):
        place = slot(which, mask)
        bit = mask & -mask
        remote(
            place, place, w_send.at[which, mask, 0], w_recv.at[which, mask], seq ^ bit, tp
        ).wait_recv()

    done_far = False
    for bit in bits:
        masks = [mask for mask in range(n) if mask & -mask == bit]
        for mask in masks:
            for which in (0, 1):
                if bit >= lowest(which):
                    arrive(which, mask)
                    forward(which, mask, slot(which, mask), bit)
            if not done_far:
                done_far = True
                piece = far.at[:, column(tp, depth)]
                remote(piece, piece, s_send.at[4], s_recv.at[4], seq ^ top, tp).wait_recv()
                for other in (1, 2, 3):
                    go(
                        remote(
                            piece, piece, s_send.at[4 + other], s_recv.at[4 + other],
                            seq, tp ^ other,
                        )
                    )
    for other in (1, 2, 3):
        for base, target in ((0, rows), (4, far)):
            piece = target.at[:, column(tp ^ other, depth)]
            remote(
                piece, piece, s_send.at[base + other], s_recv.at[base + other], seq, tp ^ other
            ).wait_recv()
    for copy in started:
        copy.wait_send()
    for copy in local:
        copy.wait()


def head_exchange(w_in, w_down, state, mod):
    n = lax.axis_size("seq")
    levels = n.bit_length() - 1
    deep, wide = w_in.shape
    tokens, depth = state.shape
    kind = jax.ShapeDtypeStruct
    anywhere = pl.BlockSpec(memory_space=pl.ANY)
    vmem = pl.BlockSpec(memory_space=pltpu.VMEM)
    dma = pltpu.SemaphoreType.DMA
    return pl.pallas_call(
        functools.partial(head_kernel, n),
        out_shape=(
            kind((n, deep, wide // 2), w_in.dtype),
            kind((n // 2, deep, wide // 2), w_down.dtype),
            kind((tokens, 4 * depth), state.dtype),
            kind((tokens, 4 * depth), state.dtype),
            kind((n,) + mod.shape, mod.dtype),
        ),
        in_specs=[anywhere, anywhere, anywhere, vmem],
        out_specs=(anywhere, anywhere, anywhere, anywhere, vmem),
        scratch_shapes=[
            pltpu.VMEM((4,) + mod.shape, mod.dtype),
            dma((3,)),
            dma((2, n, levels)),
            dma((2, n)),
            dma((8,)),
            dma((8,)),
            dma((4 + levels,)),
            dma((4 + levels,)),
        ],
        compiler_params=pltpu.CompilerParams(
            collective_id=0, has_side_effects=True, vmem_limit_bytes=16 * 1024 * 1024
        ),
    )(w_in, w_down, state, mod)


def scattered(term, axis):
    index = lax.axis_index(axis)
    core, side = index % 2, index // 2
    quarters = jnp.split(term, 4, axis=1)
    keep = [jnp.where(core == 0, quarters[i], quarters[i + 1]) for i in (0, 2)]
    give = [
        jnp.where(core == 0, quarters[i + 1], quarters[i]).astype(jnp.bfloat16) for i in (0, 2)
    ]
    got = crossed(give, axis, 1)
    low, high = [mine + other.astype(jnp.float32) for mine, other in zip(keep, got)]
    give = jnp.where(side == 0, high, low).astype(jnp.bfloat16)
    return jnp.where(side == 0, low, high) + crossed(give, axis, 2).astype(jnp.float32)


def sigma_of(step_count):
    fraction = 1.0 - step_count.astype(jnp.float32) / STEPS
    boosted = math.exp(TIME_SHIFT) * fraction
    return boosted / (boosted + 1.0 - fraction)


def time_embedding(sigma_vals):
    half_width = D // 2
    frequency = jnp.exp(-math.log(10000.0) * jnp.arange(half_width, dtype=jnp.float32) / half_width)
    phases = 1000.0 * sigma_vals[:, None] * frequency[None, :]
    return jnp.concatenate([jnp.cos(phases), jnp.sin(phases)], axis=1)


def layer_norm(rows):
    center = jnp.mean(rows, axis=-1, keepdims=True)
    spread = jnp.mean(jnp.square(rows - center), axis=-1, keepdims=True)
    return (rows - center) * lax.rsqrt(spread + NORM_EPS)


def rms_norm(rows):
    return rows * lax.rsqrt(jnp.mean(jnp.square(rows), axis=-1, keepdims=True) + NORM_EPS)


def rope_angles(id_rows):
    pieces = []
    for component, width in enumerate((HD // 8, 7 * HD // 16, 7 * HD // 16)):
        index_vec = jnp.arange(width // 2, dtype=jnp.float32)
        omega = jnp.exp(-math.log(ROPE_THETA) * 2.0 * index_vec / width)
        pieces.append(id_rows[component].astype(jnp.float32)[:, None] * omega[None, :])
    return jnp.concatenate(pieces, axis=1)


def rotate(rows, angles):
    count, heads_here, size = rows.shape
    paired = rows.reshape(count, heads_here, size // 2, 2)
    cosine = jnp.cos(angles)[:, None, :]
    sine = jnp.sin(angles)[:, None, :]
    first = paired[..., 0]
    second = paired[..., 1]
    turned = jnp.stack([first * cosine - second * sine, first * sine + second * cosine], axis=-1)
    return turned.reshape(count, heads_here, size)


def down_product(hidden_rows, weight_rows):
    return lax.dot_general(
        hidden_rows, weight_rows, (((1,), (1,)), ((), ())), preferred_element_type=jnp.float32
    )


def body(
    state,
    latent,
    w_mod,
    w_qkv,
    w_mlp_in,
    q_gain,
    k_gain,
    w_out,
    w_mlp_down,
    w_final,
    text_len,
    rope_ids,
    guidance,
    step_index,
):
    blocks = lax.axis_size("seq") // (2 * REQ)
    seq_len = TOK_DEV * blocks
    seq_index = lax.axis_index("seq")
    tp_index = lax.axis_index("tp")
    request = seq_index // (2 * blocks)
    block = seq_index // 2 % blocks
    guided_half = seq_index % 2
    width_tp = state.shape[1]
    request_pick = jnp.arange(REQ, dtype=jnp.int32) == request
    sigma_now = sigma_of(step_index)
    step_size = sigma_of(step_index + 1) - sigma_now
    time_vec = jax.nn.silu(time_embedding(sigma_now)).astype(jnp.bfloat16)
    time_rows = lax.dynamic_slice_in_dim(time_vec, tp_index * width_tp, width_tp, 1)
    partial_mod = jnp.dot(time_rows, w_mod, preferred_element_type=jnp.float32)
    final_total = jnp.sum(w_final.astype(jnp.float32), axis=0)
    mod_width = partial_mod.shape[1]
    channels = w_final.shape[1]
    extra = jnp.zeros((REQ, -(mod_width + channels) % 128), jnp.float32)
    packed = jnp.concatenate(
        [partial_mod, jnp.broadcast_to(final_total, (REQ, channels)), extra], axis=1
    )
    in_all, down_half, full_rows, far_rows, mod_all = head_exchange(
        w_mlp_in, w_mlp_down, state, packed
    )
    other_half = crossed(down_half, "seq", 1)
    modulation = mod_all[:, :, :mod_width].transpose(1, 0, 2).reshape(REQ, 3 * D)
    final_total = mod_all[0, 0, mod_width : mod_width + channels]
    own_mod = jnp.sum(jnp.where(request_pick[:, None], modulation, 0.0), axis=0)
    far_mod = jnp.sum(jnp.where(request_pick[:, None], 0.0, modulation), axis=0)
    gate_vec = lax.dynamic_slice_in_dim(own_mod[2 * D :], tp_index * width_tp, width_tp, 0)
    far_bit = lax.axis_size("seq") // 2

    def modulated(part, vec):
        rows = part.astype(jnp.float32)
        return ((1.0 + vec[D : 2 * D]) * layer_norm(rows) + vec[:D]).astype(jnp.bfloat16)

    modded = modulated(full_rows, own_mod)
    far_modded = modulated(far_rows, far_mod)
    heads_here = w_qkv.shape[2] // HD
    projected = jnp.dot(
        modded, w_qkv.reshape(D, 3 * heads_here * HD), preferred_element_type=jnp.float32
    )
    projected = projected.reshape(TOK_DEV, 3, heads_here, HD)
    mlp_pre = jnp.dot(
        jnp.concatenate([far_modded, modded], axis=0),
        in_all.reshape(D, in_all.shape[2]),
        preferred_element_type=jnp.float32,
    )
    mlp_hidden = jax.nn.gelu(mlp_pre, approximate=True).astype(jnp.bfloat16)
    even = jnp.where(guided_half == 0, down_half, other_half)
    odd = jnp.where(guided_half == 0, other_half, down_half)
    down_rows = jnp.stack([even, odd], axis=1).reshape(D, down_half.shape[2])
    far_term = down_product(mlp_hidden[:TOK_DEV], down_rows)
    mlp_term = down_product(mlp_hidden[TOK_DEV:], down_rows)
    far_update = crossed(scattered(far_term, "tp").astype(jnp.bfloat16), "seq", far_bit)
    angles = rope_angles(rope_ids)
    queries = rotate(rms_norm(projected[:, 0]) * q_gain[None], angles).astype(jnp.bfloat16)
    key_rows = rotate(rms_norm(projected[:, 1]) * k_gain[None], angles).astype(jnp.bfloat16)
    value_rows = projected[:, 2].astype(jnp.bfloat16)
    positions = block * TOK_DEV + jnp.arange(TOK_DEV, dtype=jnp.int32)
    bit_count = blocks.bit_length() - 1
    levels = range(bit_count)
    for level in levels:
        other_keys, other_values = partner((key_rows, value_rows), "seq", level + 1)
        flip_bit = block // 2**level % 2
        other_positions = positions + (1 - 2 * flip_bit) * 2**level * TOK_DEV
        key_rows = jnp.concatenate([key_rows, other_keys], axis=0)
        value_rows = jnp.concatenate([value_rows, other_values], axis=0)
        positions = jnp.concatenate([positions, other_positions], axis=0)
    flat_len = text_len.reshape(2 * REQ)
    own_len = jnp.sum(
        jnp.where(jnp.arange(2 * REQ, dtype=jnp.int32) == request * 2 + guided_half, flat_len, 0)
    )
    live = (positions >= TXT) | (positions < own_len)
    scores = jnp.einsum("qhd,khd->hqk", queries, key_rows, preferred_element_type=jnp.float32) * (
        1.0 / math.sqrt(HD)
    )
    scores = jnp.where(live[None, None, :], scores, MASKED_SCORE)
    row_max = jnp.max(scores, axis=2, keepdims=True)
    top_local = jnp.max(row_max)
    weights = jnp.exp(scores - row_max)
    weights = (weights / jnp.sum(weights, axis=2, keepdims=True)).astype(jnp.bfloat16)
    attended = jnp.einsum("hqk,khd->qhd", weights, value_rows, preferred_element_type=jnp.float32)
    attended = attended.astype(jnp.bfloat16).reshape(TOK_DEV, heads_here * HD)
    term = jnp.dot(attended, w_out, preferred_element_type=jnp.float32) + mlp_term
    update = scattered(term, "tp") + far_update.astype(jnp.float32)
    new_state = (state.astype(jnp.float32) + gate_vec * update).astype(jnp.bfloat16)
    state_values = new_state.astype(jnp.float32)
    row_total = jnp.sum(state_values, axis=1, keepdims=True)
    row_squares = jnp.sum(state_values * state_values, axis=1, keepdims=True)
    raw_velocity = jnp.dot(new_state, w_final, preferred_element_type=jnp.float32)
    peaks = jnp.where(jnp.arange(62) == tp_index, top_local, 0.0)
    tail = jnp.concatenate(
        [raw_velocity, row_total, row_squares, jnp.broadcast_to(peaks, (TOK_DEV, 62))], axis=1
    )
    tail = summed(tail, "tp")
    top_local = jnp.max(tail[0, channels + 2 : channels + 6])
    row_mean = tail[:, channels : channels + 1] / D
    row_squares = tail[:, channels + 1 : channels + 2]
    row_var = row_squares / D - row_mean * row_mean
    velocity = (tail[:, :channels] - row_mean * final_total) * lax.rsqrt(row_var + NORM_EPS)
    half_rows = TOK_DEV // 2
    keep_part = lax.dynamic_slice_in_dim(velocity, guided_half * half_rows, half_rows, 0)
    give_part = lax.dynamic_slice_in_dim(velocity, (1 - guided_half) * half_rows, half_rows, 0)
    taken_part = partner(give_part.astype(jnp.bfloat16), "seq", 0).astype(give_part.dtype)
    cond_part = jnp.where(guided_half == 0, keep_part, taken_part)
    uncond_part = jnp.where(guided_half == 0, taken_part, keep_part)
    guide_scale = jnp.sum(jnp.where(request_pick, guidance, 0)).astype(jnp.float32) / 2.0
    own_step = jnp.sum(jnp.where(request_pick, step_size, 0.0))
    next_latent = latent + own_step * (uncond_part + guide_scale * (cond_part - uncond_part))
    square_total = jnp.where(request_pick, jnp.sum(row_squares), 0.0)
    top_score = jnp.where(request_pick, top_local, MASKED_SCORE)
    mask = 1
    while mask < lax.axis_size("seq"):
        other = crossed(jnp.concatenate([square_total, top_score]), "seq", mask)
        square_total = square_total + other[:REQ]
        top_score = jnp.maximum(top_score, other[REQ:])
        mask *= 2
    state_norm = jnp.sqrt(square_total / (2.0 * seq_len * D))
    return (new_state, next_latent, state_norm, top_score)


def solution(mesh):
    in_specs = (
        P("seq", "tp"),
        P("seq", None),
        P("tp", "seq"),
        P(None, None, "tp"),
        P("seq", "tp"),
        P("tp", None),
        P("tp", None),
        P("tp", None),
        P("seq", "tp"),
        P("tp", None),
        P(),
        P(None, "seq"),
        P(),
        P(),
    )
    out_specs = (P("seq", "tp"), P("seq", None), P(), P())
    return jax.shard_map(body, mesh=mesh, in_specs=in_specs, out_specs=out_specs, check_vma=False)
```

```python
import functools
import math

import jax
import jax.numpy as jnp
from jax import lax
from jax.experimental import pallas as pl
from jax.experimental.pallas import tpu as pltpu
from jax.sharding import PartitionSpec as P

D = 3072
HD = 128
REQ = 2
TOK_DEV = 288
TXT = 512
STEPS = 28


TIME_SHIFT = 1.15
ROPE_THETA = 10000.0
NORM_EPS = 1e-06
MASKED_SCORE = -1e30


def partner(value, axis, apart):
    return lax.ppermute(value, axis, [(i, i ^ 1 << apart) for i in range(lax.axis_size(axis))])


def crossed(value, axis, mask):
    pairs = [(i, i ^ mask) for i in range(lax.axis_size(axis))]
    return jax.tree.map(lambda part: lax.ppermute(part, axis, pairs), value)


def summed(value, axis):
    mask = 1
    while mask < lax.axis_size(axis):
        value = jax.tree.map(jnp.add, value, crossed(value, axis, mask))
        mask *= 2
    return value


def head_kernel(
    n, w_in, w_down, state, mod, in_all, down_half, rows, far, mod_all, mod_parts,
    own_sem, w_send, w_recv, s_send, s_recv, m_send, m_recv,
):
    seq, tp = lax.axis_index("seq"), lax.axis_index("tp")
    top = n // 2
    side = seq // top
    width = w_in.shape[1] // 2
    depth = state.shape[1]
    bits = [1 << k for k in reversed(range(n.bit_length() - 1))]

    def column(index, size):
        return pl.ds(pl.multiple_of(index * size, size), size)

    def remote(src, dst, send, recv, to_seq, to_tp):
        return pltpu.make_async_remote_copy(
            src_ref=src, dst_ref=dst, send_sem=send, recv_sem=recv,
            device_id=(to_seq, to_tp), device_id_type=pl.DeviceIdType.MESH,
        )

    barrier = pltpu.get_barrier_semaphore()
    for bit in bits:
        pl.semaphore_signal(
            barrier, device_id=(seq ^ bit, tp), device_id_type=pl.DeviceIdType.MESH
        )
    for other in (1, 2, 3):
        pl.semaphore_signal(
            barrier, device_id=(seq, tp ^ other), device_id_type=pl.DeviceIdType.MESH
        )
    pl.semaphore_wait(barrier, len(bits) + 3)

    started = []

    def go(copy):
        copy.start()
        started.append(copy)
        return copy

    def slot(which, mask):
        return in_all.at[seq ^ mask] if which == 0 else down_half.at[(seq ^ mask) // top]

    def send_piece(which, mask, bit, src):
        return go(
            remote(
                src, slot(which, mask), w_send.at[which, mask, bit.bit_length() - 1],
                w_recv.at[which, mask | bit], seq ^ bit, tp,
            )
        )

    def lowest(which):
        return (1, top)[which]

    def forward(which, mask, src, below):
        for bit in bits:
            if lowest(which) <= bit < below:
                send_piece(which, mask, bit, src)

    for other in (1, 2, 3):
        go(remote(mod, mod_parts.at[other], m_send.at[other], m_recv.at[other], seq, tp ^ other))
    go(remote(state, far.at[:, column(tp, depth)], s_send.at[4], s_recv.at[4], seq ^ top, tp))
    for other in (1, 2, 3):
        go(
            remote(
                state, rows.at[:, column(tp, depth)], s_send.at[other], s_recv.at[other],
                seq, tp ^ other,
            )
        )
    weights = (w_in, w_down)
    for which in (0, 1):
        far_half = weights[which].at[:, column(1 - side, width)]
        near_half = weights[which].at[:, column(side, width)]
        go_far = remote(
            far_half, slot(which, 0), w_send.at[which, 0, top.bit_length() - 1],
            w_recv.at[which, top], seq ^ top, tp,
        )
        go(go_far)
        forward(which, 0, near_half, top)
    local = [
        pltpu.make_async_copy(
            weights[which].at[:, column(side, width)], slot(which, 0), own_sem.at[which]
        )
        for which in (0, 1)
    ]
    local.append(
        pltpu.make_async_copy(state, rows.at[:, column(tp, depth)], own_sem.at[2])
    )
    for copy in local:
        copy.start()

    total = mod[...]
    for other in (1, 2, 3):
        part = mod_parts.at[other]
        remote(mod, part, m_send.at[other], m_recv.at[other], seq, tp ^ other).wait_recv()
        total = total + mod_parts[other]
    mod_all[seq] = total
    for level in range(n.bit_length() - 1):
        size = 1 << level
        mine = mod_all.at[pl.ds(seq // size * size, size)]
        theirs = mod_all.at[pl.ds((seq ^ size) // size * size, size)]
        go(remote(mine, mine, m_send.at[4 + level], m_recv.at[4 + level], seq ^ size, tp))
        remote(
            mine, theirs, m_send.at[4 + level], m_recv.at[4 + level], seq ^ size, tp
        ).wait_recv()

    def arrive(which, mask):
        place = slot(which, mask)
        bit = mask & -mask
        remote(
            place, place, w_send.at[which, mask, 0], w_recv.at[which, mask], seq ^ bit, tp
        ).wait_recv()

    done_far = False
    for bit in bits:
        masks = [mask for mask in range(n) if mask & -mask == bit]
        for mask in masks:
            for which in (0, 1):
                if bit >= lowest(which):
                    arrive(which, mask)
                    forward(which, mask, slot(which, mask), bit)
            if not done_far:
                done_far = True
                piece = far.at[:, column(tp, depth)]
                remote(piece, piece, s_send.at[4], s_recv.at[4], seq ^ top, tp).wait_recv()
                for other in (1, 2, 3):
                    go(
                        remote(
                            piece, piece, s_send.at[4 + other], s_recv.at[4 + other],
                            seq, tp ^ other,
                        )
                    )
    for other in (1, 2, 3):
        for base, target in ((0, rows), (4, far)):
            piece = target.at[:, column(tp ^ other, depth)]
            remote(
                piece, piece, s_send.at[base + other], s_recv.at[base + other], seq, tp ^ other
            ).wait_recv()
    for copy in started:
        copy.wait_send()
    for copy in local:
        copy.wait()


def head_exchange(w_in, w_down, state, mod):
    n = lax.axis_size("seq")
    levels = n.bit_length() - 1
    deep, wide = w_in.shape
    tokens, depth = state.shape
    kind = jax.ShapeDtypeStruct
    anywhere = pl.BlockSpec(memory_space=pl.ANY)
    vmem = pl.BlockSpec(memory_space=pltpu.VMEM)
    dma = pltpu.SemaphoreType.DMA
    return pl.pallas_call(
        functools.partial(head_kernel, n),
        out_shape=(
            kind((n, deep, wide // 2), w_in.dtype),
            kind((2, deep, wide // 2), w_down.dtype),
            kind((tokens, 4 * depth), state.dtype),
            kind((tokens, 4 * depth), state.dtype),
            kind((n,) + mod.shape, mod.dtype),
        ),
        in_specs=[anywhere, anywhere, anywhere, vmem],
        out_specs=(anywhere, anywhere, anywhere, anywhere, vmem),
        scratch_shapes=[
            pltpu.VMEM((4,) + mod.shape, mod.dtype),
            dma((3,)),
            dma((2, n, levels)),
            dma((2, n)),
            dma((8,)),
            dma((8,)),
            dma((4 + levels,)),
            dma((4 + levels,)),
        ],
        compiler_params=pltpu.CompilerParams(
            collective_id=0, has_side_effects=True, vmem_limit_bytes=16 * 1024 * 1024
        ),
    )(w_in, w_down, state, mod)


def spread(pieces, axis, mask):
    while mask:
        for held in list(pieces):
            pieces[held | mask] = crossed(pieces[held], axis, mask)
        mask //= 2
    return pieces


def scattered(term, axis):
    index = lax.axis_index(axis)
    core, side = index % 2, index // 2
    quarters = jnp.split(term, 4, axis=1)
    keep = [jnp.where(core == 0, quarters[i], quarters[i + 1]) for i in (0, 2)]
    give = [
        jnp.where(core == 0, quarters[i + 1], quarters[i]).astype(jnp.bfloat16) for i in (0, 2)
    ]
    got = crossed(give, axis, 1)
    low, high = [mine + other.astype(jnp.float32) for mine, other in zip(keep, got)]
    give = jnp.where(side == 0, high, low).astype(jnp.bfloat16)
    return jnp.where(side == 0, low, high) + crossed(give, axis, 2).astype(jnp.float32)


def sigma_of(step_count):
    fraction = 1.0 - step_count.astype(jnp.float32) / STEPS
    boosted = math.exp(TIME_SHIFT) * fraction
    return boosted / (boosted + 1.0 - fraction)


def time_embedding(sigma_vals):
    half_width = D // 2
    frequency = jnp.exp(-math.log(10000.0) * jnp.arange(half_width, dtype=jnp.float32) / half_width)
    phases = 1000.0 * sigma_vals[:, None] * frequency[None, :]
    return jnp.concatenate([jnp.cos(phases), jnp.sin(phases)], axis=1)


def layer_norm(rows):
    center = jnp.mean(rows, axis=-1, keepdims=True)
    spread = jnp.mean(jnp.square(rows - center), axis=-1, keepdims=True)
    return (rows - center) * lax.rsqrt(spread + NORM_EPS)


def rms_norm(rows):
    return rows * lax.rsqrt(jnp.mean(jnp.square(rows), axis=-1, keepdims=True) + NORM_EPS)


def rope_angles(id_rows):
    pieces = []
    for component, width in enumerate((HD // 8, 7 * HD // 16, 7 * HD // 16)):
        index_vec = jnp.arange(width // 2, dtype=jnp.float32)
        omega = jnp.exp(-math.log(ROPE_THETA) * 2.0 * index_vec / width)
        pieces.append(id_rows[component].astype(jnp.float32)[:, None] * omega[None, :])
    return jnp.concatenate(pieces, axis=1)


def rotate(rows, angles):
    count, heads_here, size = rows.shape
    paired = rows.reshape(count, heads_here, size // 2, 2)
    cosine = jnp.cos(angles)[:, None, :]
    sine = jnp.sin(angles)[:, None, :]
    first = paired[..., 0]
    second = paired[..., 1]
    turned = jnp.stack([first * cosine - second * sine, first * sine + second * cosine], axis=-1)
    return turned.reshape(count, heads_here, size)


def down_product(hidden_rows, weight_rows):
    return lax.dot_general(
        hidden_rows, weight_rows, (((1,), (1,)), ((), ())), preferred_element_type=jnp.float32
    )


def body(
    state,
    latent,
    w_mod,
    w_qkv,
    w_mlp_in,
    q_gain,
    k_gain,
    w_out,
    w_mlp_down,
    w_final,
    text_len,
    rope_ids,
    guidance,
    step_index,
):
    blocks = lax.axis_size("seq") // (2 * REQ)
    seq_len = TOK_DEV * blocks
    seq_index = lax.axis_index("seq")
    tp_index = lax.axis_index("tp")
    request = seq_index // (2 * blocks)
    block = seq_index // 2 % blocks
    guided_half = seq_index % 2
    width_tp = state.shape[1]
    request_pick = jnp.arange(REQ, dtype=jnp.int32) == request
    sigma_now = sigma_of(step_index)
    step_size = sigma_of(step_index + 1) - sigma_now
    time_vec = jax.nn.silu(time_embedding(sigma_now)).astype(jnp.bfloat16)
    time_rows = lax.dynamic_slice_in_dim(time_vec, tp_index * width_tp, width_tp, 1)
    partial_mod = jnp.dot(time_rows, w_mod, preferred_element_type=jnp.float32)
    final_total = jnp.sum(w_final.astype(jnp.float32), axis=0)
    mod_width = partial_mod.shape[1]
    channels = w_final.shape[1]
    extra = jnp.zeros((REQ, -(mod_width + channels) % 128), jnp.float32)
    packed = jnp.concatenate(
        [partial_mod, jnp.broadcast_to(final_total, (REQ, channels)), extra], axis=1
    )
    in_all, down_half, full_rows, far_rows, mod_all = head_exchange(
        w_mlp_in, w_mlp_down, state, packed
    )
    top = lax.axis_size("seq") // 2
    down_rows = jnp.zeros((2, top) + down_half.shape[1:], down_half.dtype)
    for mask, piece in spread({0: down_half}, "seq", top // 2).items():
        down_rows = lax.dynamic_update_slice(
            down_rows, piece[:, None], (0, seq_index % top ^ mask, 0, 0)
        )
    modulation = mod_all[:, :, :mod_width].transpose(1, 0, 2).reshape(REQ, 3 * D)
    final_total = mod_all[0, 0, mod_width : mod_width + channels]
    own_mod = jnp.sum(jnp.where(request_pick[:, None], modulation, 0.0), axis=0)
    far_mod = jnp.sum(jnp.where(request_pick[:, None], 0.0, modulation), axis=0)
    gate_vec = lax.dynamic_slice_in_dim(own_mod[2 * D :], tp_index * width_tp, width_tp, 0)
    far_bit = lax.axis_size("seq") // 2

    def modulated(part, vec):
        rows = part.astype(jnp.float32)
        return ((1.0 + vec[D : 2 * D]) * layer_norm(rows) + vec[:D]).astype(jnp.bfloat16)

    modded = modulated(full_rows, own_mod)
    far_modded = modulated(far_rows, far_mod)
    heads_here = w_qkv.shape[2] // HD
    projected = jnp.dot(
        modded, w_qkv.reshape(D, 3 * heads_here * HD), preferred_element_type=jnp.float32
    )
    projected = projected.reshape(TOK_DEV, 3, heads_here, HD)
    mlp_pre = jnp.dot(
        jnp.concatenate([far_modded, modded], axis=0),
        in_all.reshape(D, in_all.shape[2]),
        preferred_element_type=jnp.float32,
    )
    mlp_hidden = jax.nn.gelu(mlp_pre, approximate=True).astype(jnp.bfloat16)
    down_rows = down_rows.reshape(D, down_half.shape[2])
    far_term = down_product(mlp_hidden[:TOK_DEV], down_rows)
    mlp_term = down_product(mlp_hidden[TOK_DEV:], down_rows)
    far_update = crossed(scattered(far_term, "tp").astype(jnp.bfloat16), "seq", far_bit)
    angles = rope_angles(rope_ids)
    queries = rotate(rms_norm(projected[:, 0]) * q_gain[None], angles).astype(jnp.bfloat16)
    key_rows = rotate(rms_norm(projected[:, 1]) * k_gain[None], angles).astype(jnp.bfloat16)
    value_rows = projected[:, 2].astype(jnp.bfloat16)
    positions = block * TOK_DEV + jnp.arange(TOK_DEV, dtype=jnp.int32)
    bit_count = blocks.bit_length() - 1
    levels = range(bit_count)
    for level in levels:
        other_keys, other_values = partner((key_rows, value_rows), "seq", level + 1)
        flip_bit = block // 2**level % 2
        other_positions = positions + (1 - 2 * flip_bit) * 2**level * TOK_DEV
        key_rows = jnp.concatenate([key_rows, other_keys], axis=0)
        value_rows = jnp.concatenate([value_rows, other_values], axis=0)
        positions = jnp.concatenate([positions, other_positions], axis=0)
    flat_len = text_len.reshape(2 * REQ)
    own_len = jnp.sum(
        jnp.where(jnp.arange(2 * REQ, dtype=jnp.int32) == request * 2 + guided_half, flat_len, 0)
    )
    live = (positions >= TXT) | (positions < own_len)
    scores = jnp.einsum("qhd,khd->hqk", queries, key_rows, preferred_element_type=jnp.float32) * (
        1.0 / math.sqrt(HD)
    )
    scores = jnp.where(live[None, None, :], scores, MASKED_SCORE)
    row_max = jnp.max(scores, axis=2, keepdims=True)
    top_local = jnp.max(row_max)
    weights = jnp.exp(scores - row_max)
    weights = (weights / jnp.sum(weights, axis=2, keepdims=True)).astype(jnp.bfloat16)
    attended = jnp.einsum("hqk,khd->qhd", weights, value_rows, preferred_element_type=jnp.float32)
    attended = attended.astype(jnp.bfloat16).reshape(TOK_DEV, heads_here * HD)
    term = jnp.dot(attended, w_out, preferred_element_type=jnp.float32) + mlp_term
    update = scattered(term, "tp") + far_update.astype(jnp.float32)
    new_state = (state.astype(jnp.float32) + gate_vec * update).astype(jnp.bfloat16)
    state_values = new_state.astype(jnp.float32)
    row_total = jnp.sum(state_values, axis=1, keepdims=True)
    row_squares = jnp.sum(state_values * state_values, axis=1, keepdims=True)
    raw_velocity = jnp.dot(new_state, w_final, preferred_element_type=jnp.float32)
    peaks = jnp.where(jnp.arange(62) == tp_index, top_local, 0.0)
    tail = jnp.concatenate(
        [raw_velocity, row_total, row_squares, jnp.broadcast_to(peaks, (TOK_DEV, 62))], axis=1
    )
    tail = summed(tail, "tp")
    top_local = jnp.max(tail[0, channels + 2 : channels + 6])
    row_mean = tail[:, channels : channels + 1] / D
    row_squares = tail[:, channels + 1 : channels + 2]
    row_var = row_squares / D - row_mean * row_mean
    velocity = (tail[:, :channels] - row_mean * final_total) * lax.rsqrt(row_var + NORM_EPS)
    half_rows = TOK_DEV // 2
    keep_part = lax.dynamic_slice_in_dim(velocity, guided_half * half_rows, half_rows, 0)
    give_part = lax.dynamic_slice_in_dim(velocity, (1 - guided_half) * half_rows, half_rows, 0)
    taken_part = partner(give_part.astype(jnp.bfloat16), "seq", 0).astype(give_part.dtype)
    cond_part = jnp.where(guided_half == 0, keep_part, taken_part)
    uncond_part = jnp.where(guided_half == 0, taken_part, keep_part)
    guide_scale = jnp.sum(jnp.where(request_pick, guidance, 0)).astype(jnp.float32) / 2.0
    own_step = jnp.sum(jnp.where(request_pick, step_size, 0.0))
    next_latent = latent + own_step * (uncond_part + guide_scale * (cond_part - uncond_part))
    square_total = jnp.where(request_pick, jnp.sum(row_squares), 0.0)
    top_score = jnp.where(request_pick, top_local, MASKED_SCORE)
    mask = 1
    while mask < lax.axis_size("seq"):
        other = crossed(jnp.concatenate([square_total, top_score]), "seq", mask)
        square_total = square_total + other[:REQ]
        top_score = jnp.maximum(top_score, other[REQ:])
        mask *= 2
    state_norm = jnp.sqrt(square_total / (2.0 * seq_len * D))
    return (new_state, next_latent, state_norm, top_score)


def solution(mesh):
    in_specs = (
        P("seq", "tp"),
        P("seq", None),
        P("tp", "seq"),
        P(None, None, "tp"),
        P("seq", "tp"),
        P("tp", None),
        P("tp", None),
        P("tp", None),
        P("seq", "tp"),
        P("tp", None),
        P(),
        P(None, "seq"),
        P(),
        P(),
    )
    out_specs = (P("seq", "tp"), P("seq", None), P(), P())
    return jax.shard_map(body, mesh=mesh, in_specs=in_specs, out_specs=out_specs, check_vma=False)
```
